256 devices in a mesh: ctx: 32 (over y, x, core), head: 8 (over z).
Axes of the slice: x: 4, y: 4, z: 8, core: 2. Of those that a mesh axis runs over, the one named last changes fastest.
Arguments:
- queries: bfloat16 [16384, 4096], P('ctx', 'head'), may hold values from -8 to 8
- keys: bfloat16 [16384, 1024], P('ctx', 'head'), may hold values from -8 to 8
- values: bfloat16 [16384, 1024], P('ctx', 'head'), may hold values from -6 to 6
- lengths: int32 [64], replicated, may hold values from 1 to 4096, 16384 in all
- out_weight: bfloat16 [4096, 4096], P(None, 'head'), may hold values from -0.09375 to 0.09375
Outputs:
- mixed: bfloat16 [16384, 4096], P('ctx', 'head')
The draws below stay inside these ranges and needn't reach their ends.
Inputs may be any that keep to these rules, and one draw needn't show every extreme that they name: `lengths`: each document holds at least one token and one holds exactly 4096; they sum to 16384.
All inputs are finite; a program needn't handle non-finite values.
Results may differ from the reference program's by a relative error of at most 0.0085.
Values may be sent and summed in bfloat16 or wider, within the bound.
A program may use at most 64 MiB of HBM per device.

```python
import math
import jax
import jax.numpy as jnp
import numpy as np
from jax import lax

D = 4096
QUERY_HEADS = 32
KEY_VALUE_HEADS = 8
HEAD_SIZE = 128
TOK_DEV = 512
PACK_TOKENS = 16384
DOCS = 64
MOST = 4096


def starting_field_name(key, heads):
    return jnp.clip(jax.random.normal(key, (PACK_TOKENS, heads, HEAD_SIZE), jnp.float32), -6.0, 6.0)


def draw_queries(key, part):
    field_name = starting_field_name(jax.random.fold_in(key, 11), QUERY_HEADS)
    return field_name.reshape(PACK_TOKENS, QUERY_HEADS * HEAD_SIZE).astype(jnp.bfloat16)


def draw_keys(key, part):
    field_name = starting_field_name(jax.random.fold_in(key, 13), KEY_VALUE_HEADS)
    return field_name.reshape(PACK_TOKENS, KEY_VALUE_HEADS * HEAD_SIZE).astype(jnp.bfloat16)


def block_scale(rng, extent, split, low, top_value):
    def one(axis_at, shards_of):
        steps = jax.random.uniform(jax.random.fold_in(jax.random.fold_in(rng, 6), axis_at), (shards_of,), jnp.float32, low / len(split), top_value / len(split))
        return jnp.repeat(jnp.exp(steps), extent[axis_at] // shards_of).reshape((-1,) + (1,) * (len(extent) - axis_at - 1))

    level = one(*split[0])
    for cut in split[1:]:
        level = level * one(*cut)
    return level


def profile(number_of, total, limit, slope):
    loads = [(1 << 20) // math.isqrt(standing ** slope) + 1 for standing in range(2, number_of + 1)]
    surplus, given = total - limit - (number_of - 1), [1] * (number_of - 1)
    while surplus > 0:
        movable = [i for i in range(number_of - 1) if given[i] < limit]
        whole, remaining = sum([loads[i] for i in movable]), surplus
        for i in movable:
            extra = min(limit - given[i], max(1, remaining * loads[i] // whole), surplus)
            given[i] = given[i] + extra
            surplus = surplus - extra
    return np.array([limit] + given)


def ragged_sizes(own_key, amount, total, reach, skew):
    if amount == 2:
        one = jax.random.randint(own_key, (), max(1, total - reach), min(reach, total - 1) + 1)
        return jnp.stack([one, total - one])
    sizes = jnp.asarray(profile(amount, total, reach, skew), jnp.int32)
    couples = (amount - 1) // 2
    source_of, sink = sizes[1:1 + 2 * couples:2], sizes[2:2 + 2 * couples:2]
    margin = jnp.minimum(source_of - 1, reach - sink)
    passed = jax.random.randint(jax.random.fold_in(own_key, 1), (couples,), 0, 1 << 20) % (margin + 1)
    sizes = sizes.at[1:1 + 2 * couples:2].set(source_of - passed).at[2:2 + 2 * couples:2].set(sink + passed)
    return sizes[jax.random.permutation(jax.random.fold_in(own_key, 2), amount)]


def gaussian(stream_key, extent, width, limit, shards=(), kind=jnp.bfloat16):
    factor_of = block_scale(stream_key, extent, shards, -0.22, 0.18) if shards else 1.0
    entries = jax.random.normal(stream_key, extent, jnp.float32) * width * factor_of
    return jnp.minimum(jnp.maximum(entries, -limit), limit).astype(kind)


def setup_inputs(seed: int = 0) -> dict:
    splits = jax.random.split(jax.random.key(seed), 6)
    return {
        "queries": draw_queries(jax.random.fold_in(splits[5], 71), 0),
        "keys": draw_keys(jax.random.fold_in(splits[5], 71), 0),
        "values": gaussian(splits[2], (PACK_TOKENS, KEY_VALUE_HEADS * HEAD_SIZE), 1.0, 6.0, ((0, 32), (1, 8))),
        "lengths": ragged_sizes(splits[3], DOCS, PACK_TOKENS, MOST, 2).astype(jnp.int32),
        "out_weight": gaussian(splits[4], (QUERY_HEADS * HEAD_SIZE, D), (QUERY_HEADS * HEAD_SIZE) ** -0.5, 0.09375, ((1, 8),)),
    }


def reference(queries, keys, values, lengths, out_weight):
    token_total_count = queries.shape[0]
    query_group_size = QUERY_HEADS // KEY_VALUE_HEADS
    window = MOST + TOK_DEV
    positions = jnp.arange(token_total_count, dtype=jnp.int32)
    boundary = jnp.cumsum(lengths)
    labels = jnp.sum((boundary[None, :] <= positions[:, None]).astype(jnp.int32), axis=1) + 1
    grouped_queries = queries.reshape(token_total_count, KEY_VALUE_HEADS, query_group_size, HEAD_SIZE)
    keyed_rows = keys.reshape(token_total_count, KEY_VALUE_HEADS, HEAD_SIZE)
    valued_rows = values.reshape(token_total_count, KEY_VALUE_HEADS, HEAD_SIZE)

    def one_block(block_index):
        q_start = (block_index * TOK_DEV).astype(jnp.int32)
        k_start = jnp.clip(q_start - MOST, 0, token_total_count - window).astype(jnp.int32)
        q_part = lax.dynamic_slice_in_dim(grouped_queries, q_start, TOK_DEV, 0).astype(jnp.float32)
        k_part = lax.dynamic_slice_in_dim(keyed_rows, k_start, window, 0).astype(jnp.float32)
        v_part = lax.dynamic_slice_in_dim(valued_rows, k_start, window, 0).astype(jnp.float32)
        q_label = lax.dynamic_slice_in_dim(labels, q_start, TOK_DEV, 0)
        k_label = lax.dynamic_slice_in_dim(labels, k_start, window, 0)
        q_pos = lax.dynamic_slice_in_dim(positions, q_start, TOK_DEV, 0)
        k_pos = lax.dynamic_slice_in_dim(positions, k_start, window, 0)
        scores = jnp.einsum("tkgd,skd->kgts", q_part, k_part) * (HEAD_SIZE ** -0.5)
        allowed = (q_label[:, None] == k_label[None, :]) & (k_pos[None, :] <= q_pos[:, None])
        scores = jnp.where(allowed, scores, -1e30)
        top = jnp.max(scores, axis=-1)
        weights = jnp.exp(scores - top[..., None])
        total = jnp.sum(weights, axis=-1)
        rounded = weights.astype(jnp.bfloat16).astype(jnp.float32)
        numer = jnp.einsum("kgts,skd->kgtd", rounded, v_part)
        attended = numer / total[..., None]
        attended = jnp.transpose(attended, (2, 0, 1, 3)).reshape(TOK_DEV, QUERY_HEADS * HEAD_SIZE)
        return attended.astype(jnp.bfloat16)

    blocks = lax.map(one_block, jnp.arange(token_total_count // TOK_DEV, dtype=jnp.int32))
    attended = blocks.reshape(token_total_count, QUERY_HEADS * HEAD_SIZE)
    return jnp.dot(attended, out_weight, preferred_element_type=jnp.float32).astype(jnp.bfloat16)
```

```python
import functools
import math

import jax
import jax.numpy as jnp
from jax import lax
from jax.experimental import pallas as pl
from jax.experimental.pallas import tpu as pltpu
from jax.sharding import PartitionSpec as P

HEAD_SIZE = 128
SCALE = HEAD_SIZE ** -0.5 * math.log2(math.e)
MASKED = -1e30
CHUNKS = 4
MESH = pl.DeviceIdType.MESH


def kernel(chips, planes, len_ref, q_hbm, k_hbm, v_hbm, w_hbm, o_ref,
           q, k_own, v_own, kb, vb, w, acc, top, first, att, gat, total,
           load_sem, kv_send, kv_recv, z_send, z_recv):
    tok = q.shape[0]
    feat = q.shape[1]
    heads = feat // HEAD_SIZE
    rows = tok // CHUNKS
    me = lax.axis_index("ctx")
    z = lax.axis_index("head")
    chip, core = me // 2, me % 2

    def peer(by):
        return {"ctx": lax.rem(chip + by + chips, chips) * 2 + core}

    sibling = {"ctx": chip * 2 + (1 - core)}
    right = {"head": lax.rem(z + 1, planes)}
    left = {"head": lax.rem(z + planes - 1, planes)}

    loads = [
        pltpu.make_async_copy(src, dst, load_sem.at[i])
        for i, (src, dst) in enumerate(((q_hbm, q), (k_hbm, k_own), (v_hbm, v_own), (w_hbm, w)))
    ]
    for c in (loads[1], loads[2], loads[0], loads[3]):
        c.start()

    barrier = pltpu.get_barrier_semaphore()
    sources = [peer(-j) for j in range(1, 5)] + [sibling, left, right]
    for d in sources:
        pl.semaphore_signal(barrier, inc=1, device_id=d, device_id_type=MESH)
    pl.semaphore_wait(barrier, len(sources))

    def kv_copies(src_k, src_v, slot, to):
        return [
            pltpu.make_async_remote_copy(
                src_ref=src, dst_ref=dst.at[slot], send_sem=kv_send.at[i, slot],
                recv_sem=kv_recv.at[i, slot], device_id=to, device_id_type=MESH)
            for i, (src, dst) in enumerate(((src_k, kb), (src_v, vb)))
        ]

    for j in (4, 3, 2, 1):
        for c in kv_copies(k_hbm, v_hbm, 2 * j - 2, peer(j)):
            c.start()
    for c in kv_copies(k_hbm, v_hbm, 8, sibling):
        c.start()

    lens = len_ref[...]
    docs = lens.shape[1]
    i0 = lax.broadcasted_iota(jnp.int32, (docs, docs), 0)
    i1 = lax.broadcasted_iota(jnp.int32, (docs, docs), 1)
    wide = jnp.broadcast_to(lens, (docs, docs))
    col = jnp.sum(jnp.where(i0 == i1, wide, 0), axis=1, keepdims=True)
    ends = jnp.sum(jnp.where(i0 <= i1, jnp.broadcast_to(col, (docs, docs)), 0), axis=0, keepdims=True)
    pos = me * tok + lax.broadcasted_iota(jnp.int32, (tok, docs), 0)
    ends = jnp.broadcast_to(ends, (tok, docs))
    began = jnp.max(jnp.where(ends <= pos, ends, 0), axis=1, keepdims=True)
    first[...] = jnp.broadcast_to(began, (tok, HEAD_SIZE))

    ones = jnp.ones((tok, HEAD_SIZE), jnp.bfloat16)
    spread = tok // HEAD_SIZE

    def attend(keys, vals, base, own):
        def one(h, carry):
            qh = q[:, pl.ds(pl.multiple_of(h * HEAD_SIZE, HEAD_SIZE), HEAD_SIZE)]
            s = lax.dot_general(qh, keys[...], (((1,), (1,)), ((), ())),
                                preferred_element_type=jnp.float32)
            at = lax.broadcasted_iota(jnp.int32, (tok, tok), 1)
            ok = at >= jnp.concatenate([first[...] - base] * spread, axis=1)
            if own:
                ok = ok & (at <= lax.broadcasted_iota(jnp.int32, (tok, tok), 0))
            s = jnp.where(ok, s, MASKED)
            new = jnp.broadcast_to(jnp.max(s, axis=1, keepdims=True), (tok, HEAD_SIZE))
            if not own:
                old = top[h]
                new = jnp.maximum(old, new)
            p = jnp.exp2((s - jnp.concatenate([new] * spread, axis=1)) * SCALE)
            both = jnp.dot(p.astype(jnp.bfloat16), jnp.concatenate([vals[...], ones], axis=1),
                           preferred_element_type=jnp.float32)
            if own:
                acc[h] = both
            else:
                fade = jnp.exp2((old - new) * SCALE)
                acc[h] = acc[h] * jnp.concatenate([fade, fade], axis=1) + both
            top[h] = new
            return carry

        lax.fori_loop(0, heads, one, 0)

    for c in loads[:3]:
        c.wait()
    attend(k_own, v_own, me * tok, True)

    for c in kv_copies(k_hbm, v_hbm, 8, sibling):
        c.wait_recv()

    def visit(n, carry):
        j, other = n // 2 + 1, n % 2
        for c in kv_copies(k_hbm, v_hbm, n, sibling):
            c.wait_recv()

        @pl.when(other == 0)
        def _():
            for c in kv_copies(kb.at[n], vb.at[n], n + 1, sibling):
                c.start()

        slot = jnp.where((n == 7) & (core == 1), 8, n)
        whose = jnp.where(other == 0, core, 1 - core)
        block = jnp.where(slot == 8, chip * 2, (chip - j) * 2 + whose)
        attend(kb.at[slot], vb.at[slot], block * tok, False)
        return carry

    lax.fori_loop(0, 8, visit, 0)

    def z_copy(src, t, slot, to):
        return pltpu.make_async_remote_copy(
            src_ref=src, dst_ref=gat.at[t, slot], send_sem=z_send.at[t, slot],
            recv_sem=z_recv.at[t, slot], device_id=to, device_id_type=MESH)

    last = planes - 2
    for t in range(CHUNKS):
        span = pl.ds(t * rows, rows)
        for h in range(heads):
            num = acc[h, span, 0:HEAD_SIZE]
            den = acc[h, span, HEAD_SIZE:2 * HEAD_SIZE]
            att[t, :, h * HEAD_SIZE:(h + 1) * HEAD_SIZE] = (num / den).astype(jnp.bfloat16)
        z_copy(att.at[t], t, 0, right).start()
        z_copy(att.at[t], t, last, left).start()

    def weight(by):
        plane = lax.rem(z + planes - by, planes)
        return w[pl.ds(pl.multiple_of(plane * feat, feat), feat), :]

    loads[3].wait()
    for t in range(CHUNKS):
        total[pl.ds(t * rows, rows), :] = jnp.dot(att[t], weight(0), preferred_element_type=jnp.float32)

    def add(t, slot):
        total[pl.ds(t * rows, rows), :] += jnp.dot(
            gat[t, slot], weight(slot + 1), preferred_element_type=jnp.float32)

    half = planes // 2
    for d in range(1, half + 1):
        for t in range(CHUNKS):
            far_right = half - t % 2
            far_left = planes - 1 - far_right
            if d <= far_right:
                z_copy(att.at[t], t, d - 1, right).wait_recv()
                if d < far_right:
                    z_copy(gat.at[t, d - 1], t, d, right).start()
            if d <= far_left:
                s = planes - 1 - d
                z_copy(att.at[t], t, s, left).wait_recv()
                if d < far_left:
                    z_copy(gat.at[t, s], t, s - 1, left).start()
            if d <= far_right:
                add(t, d - 1)
            if d <= far_left:
                add(t, planes - 1 - d)
    o_ref[...] = total[...].astype(o_ref.dtype)

    for slot in range(9):
        for c in kv_copies(k_hbm, v_hbm, slot, sibling):
            c.wait_send()
    for t in range(CHUNKS):
        for slot in range(planes - 1):
            z_copy(att.at[t], t, slot, right).wait_send()


def shards(chips, planes, queries, keys, values, lengths, out_weight):
    tok, feat = queries.shape
    heads = feat // HEAD_SIZE
    bf, f32 = jnp.bfloat16, jnp.float32
    rows = tok // CHUNKS
    hbm = pl.BlockSpec(memory_space=pl.ANY)
    return pl.pallas_call(
        functools.partial(kernel, chips, planes),
        out_shape=jax.ShapeDtypeStruct((tok, out_weight.shape[1]), bf),
        in_specs=[pl.BlockSpec(memory_space=pltpu.VMEM), hbm, hbm, hbm, hbm],
        out_specs=pl.BlockSpec(memory_space=pltpu.VMEM),
        scratch_shapes=[
            pltpu.VMEM((tok, feat), bf),
            pltpu.VMEM((tok, HEAD_SIZE), bf),
            pltpu.VMEM((tok, HEAD_SIZE), bf),
            pltpu.VMEM((9, tok, HEAD_SIZE), bf),
            pltpu.VMEM((9, tok, HEAD_SIZE), bf),
            pltpu.VMEM(out_weight.shape, bf),
            pltpu.VMEM((heads, tok, 2 * HEAD_SIZE), f32),
            pltpu.VMEM((heads, tok, HEAD_SIZE), f32),
            pltpu.VMEM((tok, HEAD_SIZE), jnp.int32),
            pltpu.VMEM((CHUNKS, rows, feat), bf),
            pltpu.VMEM((CHUNKS, planes - 1, rows, feat), bf),
            pltpu.VMEM((tok, out_weight.shape[1]), f32),
            pltpu.SemaphoreType.DMA((4,)),
            pltpu.SemaphoreType.DMA((2, 9)),
            pltpu.SemaphoreType.DMA((2, 9)),
            pltpu.SemaphoreType.DMA((CHUNKS, planes - 1)),
            pltpu.SemaphoreType.DMA((CHUNKS, planes - 1)),
        ],
        compiler_params=pltpu.CompilerParams(
            collective_id=0, has_side_effects=True, vmem_limit_bytes=62 * 2**20),
    )(lengths.reshape(1, -1), queries, keys, values, out_weight)


def solution(mesh):
    return jax.shard_map(
        functools.partial(shards, mesh.shape["ctx"] // 2, mesh.shape["head"]),
        mesh=mesh,
        in_specs=(P("ctx", "head"), P("ctx", "head"), P("ctx", "head"), P(), P(None, "head")),
        out_specs=P("ctx", "head"),
        check_vma=False,
    )
```

```python
import functools
import math

import jax
import jax.numpy as jnp
from jax import lax
from jax.experimental import pallas as pl
from jax.experimental.pallas import tpu as pltpu
from jax.sharding import PartitionSpec as P

HEAD_SIZE = 128
SCALE = HEAD_SIZE ** -0.5 * math.log2(math.e)
MASKED = -1e30
CHUNKS = 4
ROW = 4
SAME = {2: 0, 3: 2, 1: 4, 4: 6}
MATE = 8
MESH = pl.DeviceIdType.MESH


def kernel(chips, planes, len_ref, q_hbm, k_hbm, v_hbm, w_hbm, o_ref,
           q, k_own, v_own, kb, vb, w, acc, top, first, bias, tail, att, gat, total,
           load_sem, kv_send, kv_recv, z_send, z_recv):
    tok = q.shape[0]
    feat = q.shape[1]
    heads = feat // HEAD_SIZE
    rows = tok // CHUNKS
    me = lax.axis_index("ctx")
    z = lax.axis_index("head")
    chip, core = me // 2, me % 2
    x = chip % ROW

    def at_chip(c):
        return {"ctx": c * 2 + core}

    below = at_chip(lax.rem(chip + ROW, chips))
    above = at_chip(lax.rem(chip + chips - ROW, chips))
    east = at_chip(chip - x + lax.rem(x + 1, ROW))
    west = at_chip(chip - x + lax.rem(x + ROW - 1, ROW))
    sibling = {"ctx": chip * 2 + (1 - core)}
    right = {"head": lax.rem(z + 1, planes)}
    left = {"head": lax.rem(z + planes - 1, planes)}

    loads = [
        pltpu.make_async_copy(src, dst, load_sem.at[i])
        for i, (src, dst) in enumerate(((q_hbm, q), (k_hbm, k_own), (v_hbm, v_own), (w_hbm, w)))
    ]
    for c in (loads[1], loads[2], loads[0], loads[3]):
        c.start()

    barrier = pltpu.get_barrier_semaphore()
    sources = [above, east, west, sibling, left, right]
    for d in sources:
        pl.semaphore_signal(barrier, inc=1, device_id=d, device_id_type=MESH)
    pl.semaphore_wait(barrier, len(sources))

    own = (k_hbm, v_hbm)
    held = (kb, vb)

    def send(i, src, slot, sem, to):
        return pltpu.make_async_remote_copy(
            src_ref=src, dst_ref=held[i].at[slot], send_sem=kv_send.at[i, sem],
            recv_sem=kv_recv.at[i, slot], device_id=to, device_id_type=MESH)

    def arrive(i, slot):
        send(i, own[i], slot, 0, sibling).wait_recv()

    def to_mate(i, j):
        return send(i, held[i].at[SAME[j]], SAME[j] + 1, 5 + j, sibling)

    for i in range(2):
        send(i, own[i], SAME[4], 0, below).start()

        @pl.when(x < ROW - 1)
        def _():
            send(i, own[i], SAME[1], 1, east).start()

        @pl.when(x == 0)
        def _():
            send(i, own[i], SAME[3], 3, west).start()

    for i in range(2):
        send(i, own[i], MATE, 5, sibling).start()

    lens = len_ref[...]
    docs = lens.shape[1]
    i0 = lax.broadcasted_iota(jnp.int32, (docs, docs), 0)
    i1 = lax.broadcasted_iota(jnp.int32, (docs, docs), 1)
    wide = jnp.broadcast_to(lens, (docs, docs))
    col = jnp.sum(jnp.where(i0 == i1, wide, 0), axis=1, keepdims=True)
    ends = jnp.sum(jnp.where(i0 <= i1, jnp.broadcast_to(col, (docs, docs)), 0), axis=0, keepdims=True)
    pos = me * tok + lax.broadcasted_iota(jnp.int32, (tok, docs), 0)
    ends = jnp.broadcast_to(ends, (tok, docs))
    began = jnp.max(jnp.where(ends <= pos, ends, 0), axis=1, keepdims=True)
    first[...] = jnp.broadcast_to(began, (tok, HEAD_SIZE))

    spread = tok // HEAD_SIZE

    def limits(r0, m, bases, causal):
        parts = []
        lane = lax.broadcasted_iota(jnp.int32, (m, tok), 1)
        for base in bases:
            ok = lane >= jnp.concatenate([first[r0:r0 + m, :] - base] * spread, axis=1)
            if causal:
                ok = ok & (lane <= lax.broadcasted_iota(jnp.int32, (m, tok), 0))
            parts.append(jnp.where(ok, jnp.float32(-MASKED), jnp.float32(MASKED)))
        return parts[0] if len(parts) == 1 else jnp.concatenate(parts, axis=1)

    def attend(r0, m, keys, vals, limit, fresh):
        wide = keys.shape[0]
        vals = jnp.concatenate([vals, jnp.ones((wide, HEAD_SIZE), jnp.bfloat16)], axis=1)
        span = slice(r0, r0 + m)

        def score(h):
            return lax.dot_general(q[span, h * HEAD_SIZE:(h + 1) * HEAD_SIZE], keys, (((1,), (1,)), ((), ())),
                                   preferred_element_type=jnp.float32)

        ahead = score(0)
        for h in range(heads):
            s = ahead
            if h + 1 < heads:
                ahead = score(h + 1)
            s = jnp.minimum(s, limit[...])
            new = jnp.broadcast_to(jnp.max(s, axis=1, keepdims=True), (m, HEAD_SIZE))
            if not fresh:
                old = top[h, span, :]
                new = jnp.maximum(old, new)
            p = jnp.exp2((s - jnp.concatenate([new] * (wide // HEAD_SIZE), axis=1)) * SCALE)
            both = jnp.dot(p.astype(jnp.bfloat16), vals, preferred_element_type=jnp.float32)
            if fresh:
                acc[h, span, :] = both
            else:
                fade = jnp.exp2((old - new) * SCALE)
                acc[h, span, :] = acc[h, span, :] * jnp.concatenate([fade, fade], axis=1) + both
            top[h, span, :] = new

    for c in loads[:3]:
        c.wait()
    bias[...] = limits(0, tok, [me * tok], True)
    attend(0, tok, k_own[...], v_own[...], bias, True)

    for i in range(2):
        arrive(i, SAME[4])

        @pl.when(x == ROW - 1)
        def _():
            send(i, held[i].at[SAME[4]], SAME[1], 1, east).start()

        @pl.when(x > 0)
        def _():
            send(i, held[i].at[SAME[4]], SAME[3], 3, west).start()

        to_mate(i, 4).start()
    for i in range(2):
        arrive(i, SAME[1])

        @pl.when((x < ROW - 1) if i == 0 else (x == ROW - 2))
        def _():
            send(i, held[i].at[SAME[1]], SAME[2], 2, east).start()

        to_mate(i, 1).start()

    def from_row(i):
        arrive(i, SAME[3])

        @pl.when((x == 1) if i == 0 else (x > 0))
        def _():
            send(i, held[i].at[SAME[3]], SAME[2], 4, west).start()

        to_mate(i, 3).start()

    from_row(0)
    for i in range(2):
        arrive(i, MATE)
        arrive(i, SAME[4] + 1)

    def far(n, carry):
        mine = jnp.where(core == 1, MATE, SAME[4] + 1)
        slot = jnp.where(n == 0, SAME[4], mine)
        block = jnp.where(n == 0, (chip - 4) * 2 + core, jnp.where(core == 1, chip * 2, (chip - 4) * 2 + 1))
        bias[...] = limits(0, tok, [block * tok], False)
        attend(0, tok, kb[slot], vb[slot], bias, False)
        return carry

    lax.fori_loop(0, 2, far, 0)
    from_row(1)
    for i in range(2):
        arrive(i, SAME[1] + 1)

    def near(n, carry):
        block = (chip - 1) * 2 + jnp.where(n == 0, core, 1 - core)
        bias[...] = limits(0, tok, [block * tok], False)
        attend(0, tok, kb[SAME[1] + n], vb[SAME[1] + n], bias, False)
        arrive_mid(n)
        return carry

    def arrive_mid(n):
        for i in range(2):
            @pl.when(n == i)
            def _():
                arrive(i, SAME[2])
                to_mate(i, 2).start()

    lax.fori_loop(0, 2, near, 0)
    for i in range(2):
        arrive(i, SAME[3] + 1)
        arrive(i, SAME[2] + 1)

    def z_copy(src, t, slot, to):
        return pltpu.make_async_remote_copy(
            src_ref=src, dst_ref=gat.at[t, slot], send_sem=z_send.at[t, slot],
            recv_sem=z_recv.at[t, slot], device_id=to, device_id_type=MESH)

    last = planes - 2
    bases = [((chip - j) * 2 + c) * tok for j in (2, 3) for c in (core, 1 - core)]
    late = len(bases)
    for t in range(CHUNKS):
        tail[...] = limits(t * rows, rows, bases, False)
        attend(t * rows, rows, kb[0:late].reshape(late * tok, HEAD_SIZE), vb[0:late].reshape(late * tok, HEAD_SIZE),
               tail, False)
        span = pl.ds(t * rows, rows)
        for h in range(heads):
            num = acc[h, span, 0:HEAD_SIZE]
            den = acc[h, span, HEAD_SIZE:2 * HEAD_SIZE]
            att[t, :, h * HEAD_SIZE:(h + 1) * HEAD_SIZE] = (num / den).astype(jnp.bfloat16)
        z_copy(att.at[t], t, 0, right).start()
        z_copy(att.at[t], t, last, left).start()

    def weight(by):
        plane = lax.rem(z + planes - by, planes)
        return w[pl.ds(pl.multiple_of(plane * feat, feat), feat), :]

    loads[3].wait()
    for t in range(CHUNKS):
        total[pl.ds(t * rows, rows), :] = jnp.dot(att[t], weight(0), preferred_element_type=jnp.float32)

    def add(t, slot):
        total[pl.ds(t * rows, rows), :] += jnp.dot(
            gat[t, slot], weight(slot + 1), preferred_element_type=jnp.float32)

    half = planes // 2
    for d in range(1, half + 1):
        for t in range(CHUNKS):
            far_right = half - t % 2
            far_left = planes - 1 - far_right
            if d <= far_right:
                z_copy(att.at[t], t, d - 1, right).wait_recv()
                if d < far_right:
                    z_copy(gat.at[t, d - 1], t, d, right).start()
            if d <= far_left:
                s = planes - 1 - d
                z_copy(att.at[t], t, s, left).wait_recv()
                if d < far_left:
                    z_copy(gat.at[t, s], t, s - 1, left).start()
            if d <= far_right:
                add(t, d - 1)
            if d <= far_left:
                add(t, planes - 1 - d)
    o_ref[...] = total[...].astype(o_ref.dtype)

    def sent(i, sem):
        send(i, own[i], MATE, sem, sibling).wait_send()

    for i in range(2):
        for sem in (0, 1, 3, 5, 6, 7, 8, 9):
            sent(i, sem)

        @pl.when((x < ROW - 1) if i == 0 else (x == ROW - 2))
        def _():
            sent(i, 2)

        @pl.when((x == 1) if i == 0 else (x > 0))
        def _():
            sent(i, 4)

    for t in range(CHUNKS):
        for slot in range(planes - 1):
            z_copy(att.at[t], t, slot, right).wait_send()


def shards(chips, planes, queries, keys, values, lengths, out_weight):
    tok, feat = queries.shape
    heads = feat // HEAD_SIZE
    bf, f32 = jnp.bfloat16, jnp.float32
    rows = tok // CHUNKS
    hbm = pl.BlockSpec(memory_space=pl.ANY)
    return pl.pallas_call(
        functools.partial(kernel, chips, planes),
        out_shape=jax.ShapeDtypeStruct((tok, out_weight.shape[1]), bf),
        in_specs=[pl.BlockSpec(memory_space=pltpu.VMEM), hbm, hbm, hbm, hbm],
        out_specs=pl.BlockSpec(memory_space=pltpu.VMEM),
        scratch_shapes=[
            pltpu.VMEM((tok, feat), bf),
            pltpu.VMEM((tok, HEAD_SIZE), bf),
            pltpu.VMEM((tok, HEAD_SIZE), bf),
            pltpu.VMEM((9, tok, HEAD_SIZE), bf),
            pltpu.VMEM((9, tok, HEAD_SIZE), bf),
            pltpu.VMEM(out_weight.shape, bf),
            pltpu.VMEM((heads, tok, 2 * HEAD_SIZE), f32),
            pltpu.VMEM((heads, tok, HEAD_SIZE), f32),
            pltpu.VMEM((tok, HEAD_SIZE), jnp.int32),
            pltpu.VMEM((tok, tok), f32),
            pltpu.VMEM((rows, 4 * tok), f32),
            pltpu.VMEM((CHUNKS, rows, feat), bf),
            pltpu.VMEM((CHUNKS, planes - 1, rows, feat), bf),
            pltpu.VMEM((tok, out_weight.shape[1]), f32),
            pltpu.SemaphoreType.DMA((4,)),
            pltpu.SemaphoreType.DMA((2, 10)),
            pltpu.SemaphoreType.DMA((2, 9)),
            pltpu.SemaphoreType.DMA((CHUNKS, planes - 1)),
            pltpu.SemaphoreType.DMA((CHUNKS, planes - 1)),
        ],
        compiler_params=pltpu.CompilerParams(
            collective_id=0, has_side_effects=True, vmem_limit_bytes=62 * 2**20),
    )(lengths.reshape(1, -1), queries, keys, values, out_weight)


def solution(mesh):
    return jax.shard_map(
        functools.partial(shards, mesh.shape["ctx"] // 2, mesh.shape["head"]),
        mesh=mesh,
        in_specs=(P("ctx", "head"), P("ctx", "head"), P("ctx", "head"), P(), P(None, "head")),
        out_specs=P("ctx", "head"),
        check_vma=False,
    )
```

```python
import functools
import math

import jax
import jax.numpy as jnp
from jax import lax
from jax.experimental import pallas as pl
from jax.experimental.pallas import tpu as pltpu
from jax.sharding import PartitionSpec as P

HEAD_SIZE = 128
SCALE = HEAD_SIZE ** -0.5 * math.log2(math.e)
MASKED = -1e30
CHUNKS = 4
ROW = 4
PIECES = 2
SAME = {2: 0, 3: 2, 1: 4, 4: 6}
MATE = 8
MESH = pl.DeviceIdType.MESH


def kernel(chips, planes, len_ref, q_hbm, k_hbm, v_hbm, w_hbm, o_ref,
           q, k_own, v_own, kb, vb, w, acc, top, first, bias, tail, att, gat, total, out,
           load_sem, kv_send, kv_recv, z_send, z_recv, out_sem):
    tok = q.shape[0]
    feat = q.shape[1]
    heads = feat // HEAD_SIZE
    rows = tok // CHUNKS
    me = lax.axis_index("ctx")
    z = lax.axis_index("head")
    chip, core = me // 2, me % 2
    x = chip % ROW

    def at_chip(c):
        return {"ctx": c * 2 + core}

    below = at_chip(lax.rem(chip + ROW, chips))
    above = at_chip(lax.rem(chip + chips - ROW, chips))
    peers = [at_chip(chip - x + lax.rem(x + j, ROW)) for j in range(1, ROW)]
    ahead_two = at_chip(lax.rem(chip + 2, chips))
    behind_two = at_chip(lax.rem(chip + chips - 2, chips))
    sibling = {"ctx": chip * 2 + (1 - core)}
    right = {"head": lax.rem(z + 1, planes)}
    left = {"head": lax.rem(z + planes - 1, planes)}

    loads = [
        pltpu.make_async_copy(src, dst, load_sem.at[i])
        for i, (src, dst) in enumerate(((q_hbm, q), (k_hbm, k_own), (v_hbm, v_own), (w_hbm, w)))
    ]
    for c in (loads[1], loads[2], loads[0], loads[3]):
        c.start()

    barrier = pltpu.get_barrier_semaphore()
    sources = [above, *peers, behind_two, sibling, left, right]
    for d in sources:
        pl.semaphore_signal(barrier, inc=1, device_id=d, device_id_type=MESH)
    pl.semaphore_wait(barrier, len(sources))

    part = tok // PIECES
    pieces = range(2 * PIECES)

    def piece(refs, i, *at):
        return refs[i // PIECES].at[(*at, pl.ds(i % PIECES * part, part))]

    def send(i, src, slot, sem, to):
        return pltpu.make_async_remote_copy(
            src_ref=src, dst_ref=piece((kb, vb), i, slot), send_sem=kv_send.at[i, sem],
            recv_sem=kv_recv.at[i, slot], device_id=to, device_id_type=MESH)

    def own(i):
        return piece((k_hbm, v_hbm), i)

    def arrive(i, slot):
        send(i, own(i), slot, 0, sibling).wait_recv()

    def from_chip(i, j):
        arrive(i, SAME[j])
        send(i, piece((kb, vb), i, SAME[j]), SAME[j] + 1, 5 + j, sibling).start()

    for i in pieces:
        send(i, own(i), SAME[4], 0, below).start()
        for j in (1, 3, 2):
            @pl.when(x + j < ROW)
            def _():
                send(i, own(i), SAME[j], j, peers[j - 1]).start()

    @pl.when(x == ROW - 2)
    def _():
        for i in pieces:
            send(i, own(i), SAME[2], 2, ahead_two).start()

    @pl.when(x == ROW - 1)
    def _():
        for i in pieces[PIECES:]:
            send(i, own(i), SAME[2], 2, ahead_two).start()

    for i in pieces:
        send(i, own(i), MATE, 5, sibling).start()

    lens = len_ref[...]
    docs = lens.shape[1]
    i0 = lax.broadcasted_iota(jnp.int32, (docs, docs), 0)
    i1 = lax.broadcasted_iota(jnp.int32, (docs, docs), 1)
    wide = jnp.broadcast_to(lens, (docs, docs))
    col = jnp.sum(jnp.where(i0 == i1, wide, 0), axis=1, keepdims=True)
    ends = jnp.sum(jnp.where(i0 <= i1, jnp.broadcast_to(col, (docs, docs)), 0), axis=0, keepdims=True)
    pos = me * tok + lax.broadcasted_iota(jnp.int32, (tok, docs), 0)
    ends = jnp.broadcast_to(ends, (tok, docs))
    began = jnp.max(jnp.where(ends <= pos, ends, 0), axis=1, keepdims=True)
    first[...] = jnp.broadcast_to(began, (tok, HEAD_SIZE))

    spread = tok // HEAD_SIZE

    def limits(r0, m, bases, causal):
        parts = []
        lane = lax.broadcasted_iota(jnp.int32, (m, tok), 1)
        for base in bases:
            ok = lane >= jnp.concatenate([first[r0:r0 + m, :] - base] * spread, axis=1)
            if causal:
                ok = ok & (lane <= lax.broadcasted_iota(jnp.int32, (m, tok), 0))
            parts.append(jnp.where(ok, jnp.float32(-MASKED), jnp.float32(MASKED)))
        return parts[0] if len(parts) == 1 else jnp.concatenate(parts, axis=1)

    def attend(r0, m, keys, vals, limit, fresh):
        wide = keys.shape[0]
        vals = jnp.concatenate([vals, jnp.ones((wide, HEAD_SIZE), jnp.bfloat16)], axis=1)
        span = slice(r0, r0 + m)

        def score(h):
            return lax.dot_general(q[span, h * HEAD_SIZE:(h + 1) * HEAD_SIZE], keys, (((1,), (1,)), ((), ())),
                                   preferred_element_type=jnp.float32)

        ahead = score(0)
        for h in range(heads):
            s = ahead
            if h + 1 < heads:
                ahead = score(h + 1)
            s = jnp.minimum(s, limit[...])
            new = jnp.broadcast_to(jnp.max(s, axis=1, keepdims=True), (m, HEAD_SIZE))
            if not fresh:
                old = top[h, span, :]
                new = jnp.maximum(old, new)
            p = jnp.exp2((s - jnp.concatenate([new] * (wide // HEAD_SIZE), axis=1)) * SCALE)
            both = jnp.dot(p.astype(jnp.bfloat16), vals, preferred_element_type=jnp.float32)
            if fresh:
                acc[h, span, :] = both
            else:
                fade = jnp.exp2((old - new) * SCALE)
                acc[h, span, :] = acc[h, span, :] * jnp.concatenate([fade, fade], axis=1) + both
            top[h, span, :] = new

    for c in loads[:3]:
        c.wait()
    bias[...] = limits(0, tok, [me * tok], True)
    attend(0, tok, k_own[...], v_own[...], bias, True)

    for i in pieces:
        arrive(i, SAME[4])
        for j in (3, 1, 2)[:3 if i < PIECES else 2]:
            @pl.when((x + j >= ROW) if j != 2 else (x == ROW - 1))
            def _():
                send(i, piece((kb, vb), i, SAME[4]), SAME[j], j, peers[j - 1]).start()
    for i in pieces:
        send(i, piece((kb, vb), i, SAME[4]), SAME[4] + 1, 9, sibling).start()
    for i in pieces:
        arrive(i, MATE)
        arrive(i, SAME[4] + 1)

    def far(n, carry):
        mine = jnp.where(core == 1, MATE, SAME[4] + 1)
        slot = jnp.where(n == 0, SAME[4], mine)
        block = jnp.where(n == 0, (chip - 4) * 2 + core, jnp.where(core == 1, chip * 2, (chip - 4) * 2 + 1))
        bias[...] = limits(0, tok, [block * tok], False)
        attend(0, tok, kb[slot], vb[slot], bias, False)
        return carry

    lax.fori_loop(0, 2, far, 0)
    for j in (1, 3, 2):
        for i in pieces:
            from_chip(i, j)

    def z_copy(src, t, slot, to):
        return pltpu.make_async_remote_copy(
            src_ref=src, dst_ref=gat.at[t, slot], send_sem=z_send.at[t, slot],
            recv_sem=z_recv.at[t, slot], device_id=to, device_id_type=MESH)

    last = planes - 2
    bases = [((chip - j) * 2 + c) * tok for j in (2, 3, 1) for c in (core, 1 - core)]

    def attend_slots(t, low, high):
        wide = (high - low) * tok
        limit = tail.at[:, low * tok:high * tok]
        limit[...] = limits(t * rows, rows, bases[low:high], False)
        attend(t * rows, rows, kb[low:high].reshape(wide, HEAD_SIZE), vb[low:high].reshape(wide, HEAD_SIZE), limit, False)

    for t in range(CHUNKS):
        if t == 0:
            for i in pieces:
                arrive(i, SAME[1] + 1)
            attend_slots(t, 4, 6)
            for i in pieces:
                arrive(i, SAME[3] + 1)
                arrive(i, SAME[2] + 1)
            attend_slots(t, 0, 4)
        else:
            attend_slots(t, 0, 6)
        span = pl.ds(t * rows, rows)
        for h in range(heads):
            num = acc[h, span, 0:HEAD_SIZE]
            den = acc[h, span, HEAD_SIZE:2 * HEAD_SIZE]
            att[t, :, h * HEAD_SIZE:(h + 1) * HEAD_SIZE] = (num / den).astype(jnp.bfloat16)
        z_copy(att.at[t], t, 0, right).start()
        z_copy(att.at[t], t, last, left).start()

    def weight(by):
        plane = lax.rem(z + planes - by, planes)
        return w[pl.ds(pl.multiple_of(plane * feat, feat), feat), :]

    loads[3].wait()
    for t in range(CHUNKS):
        total[pl.ds(t * rows, rows), :] = jnp.dot(att[t], weight(0), preferred_element_type=jnp.float32)

    def add(t, slot):
        total[pl.ds(t * rows, rows), :] += jnp.dot(
            gat[t, slot], weight(slot + 1), preferred_element_type=jnp.float32)

    def out_copy(t):
        span = pl.ds(t * rows, rows)
        return pltpu.make_async_copy(out.at[span], o_ref.at[span], out_sem.at[t])

    half = planes // 2
    for d in range(1, half + 1):
        for t in range(CHUNKS):
            far_right = half - t % 2
            far_left = planes - 1 - far_right
            if d <= far_right:
                z_copy(att.at[t], t, d - 1, right).wait_recv()
                if d < far_right:
                    z_copy(gat.at[t, d - 1], t, d, right).start()
            if d <= far_left:
                s = planes - 1 - d
                z_copy(att.at[t], t, s, left).wait_recv()
                if d < far_left:
                    z_copy(gat.at[t, s], t, s - 1, left).start()
            if d <= far_right:
                add(t, d - 1)
            if d <= far_left:
                add(t, planes - 1 - d)
            if d == half:
                span = pl.ds(t * rows, rows)
                out[span, :] = total[span, :].astype(out.dtype)
                out_copy(t).start()
    for t in range(CHUNKS):
        out_copy(t).wait()

    for i in pieces:
        for sem in (0, 1, 2, 3, 5, 6, 7, 8, 9):
            send(i, own(i), MATE, sem, sibling).wait_send()
    for t in range(CHUNKS):
        for slot in range(planes - 1):
            z_copy(att.at[t], t, slot, right).wait_send()


def shards(chips, planes, queries, keys, values, lengths, out_weight):
    tok, feat = queries.shape
    heads = feat // HEAD_SIZE
    bf, f32 = jnp.bfloat16, jnp.float32
    rows = tok // CHUNKS
    hbm = pl.BlockSpec(memory_space=pl.ANY)
    return pl.pallas_call(
        functools.partial(kernel, chips, planes),
        out_shape=jax.ShapeDtypeStruct((tok, out_weight.shape[1]), bf),
        in_specs=[pl.BlockSpec(memory_space=pltpu.VMEM), hbm, hbm, hbm, hbm],
        out_specs=hbm,
        scratch_shapes=[
            pltpu.VMEM((tok, feat), bf),
            pltpu.VMEM((tok, HEAD_SIZE), bf),
            pltpu.VMEM((tok, HEAD_SIZE), bf),
            pltpu.VMEM((9, tok, HEAD_SIZE), bf),
            pltpu.VMEM((9, tok, HEAD_SIZE), bf),
            pltpu.VMEM(out_weight.shape, bf),
            pltpu.VMEM((heads, tok, 2 * HEAD_SIZE), f32),
            pltpu.VMEM((heads, tok, HEAD_SIZE), f32),
            pltpu.VMEM((tok, HEAD_SIZE), jnp.int32),
            pltpu.VMEM((tok, tok), f32),
            pltpu.VMEM((rows, 6 * tok), f32),
            pltpu.VMEM((CHUNKS, rows, feat), bf),
            pltpu.VMEM((CHUNKS, planes - 1, rows, feat), bf),
            pltpu.VMEM((tok, out_weight.shape[1]), f32),
            pltpu.VMEM((tok, out_weight.shape[1]), bf),
            pltpu.SemaphoreType.DMA((4,)),
            pltpu.SemaphoreType.DMA((2 * PIECES, 10)),
            pltpu.SemaphoreType.DMA((2 * PIECES, 9)),
            pltpu.SemaphoreType.DMA((CHUNKS, planes - 1)),
            pltpu.SemaphoreType.DMA((CHUNKS, planes - 1)),
            pltpu.SemaphoreType.DMA((CHUNKS,)),
        ],
        compiler_params=pltpu.CompilerParams(
            collective_id=0, has_side_effects=True, vmem_limit_bytes=62 * 2**20),
    )(lengths.reshape(1, -1), queries, keys, values, out_weight)


def solution(mesh):
    return jax.shard_map(
        functools.partial(shards, mesh.shape["ctx"] // 2, mesh.shape["head"]),
        mesh=mesh,
        in_specs=(P("ctx", "head"), P("ctx", "head"), P("ctx", "head"), P(), P(None, "head")),
        out_specs=P("ctx", "head"),
        check_vma=False,
    )
```

```python
import functools
import math

import jax
import jax.numpy as jnp
from jax import lax
from jax.experimental import pallas as pl
from jax.experimental.pallas import tpu as pltpu
from jax.sharding import PartitionSpec as P

HEAD_SIZE = 128
SCALE = HEAD_SIZE ** -0.5 * math.log2(math.e)
MASKED = -1e30
CHUNKS = 4
ROW = 4
PIECES = 2
SAME = {2: 0, 3: 2, 1: 4, 4: 6}
MATE = 8
MESH = pl.DeviceIdType.MESH


def kernel(chips, planes, len_ref, q_hbm, k_hbm, v_hbm, w_hbm, o_ref,
           q, k_own, v_own, kb, vb, w, acc, top, first, bias, tail, att, gat, total, out,
           load_sem, kv_send, kv_recv, z_send, z_recv, out_sem):
    tok = q.shape[0]
    feat = q.shape[1]
    heads = feat // HEAD_SIZE
    rows = tok // CHUNKS
    me = lax.axis_index("ctx")
    z = lax.axis_index("head")
    chip, core = me // 2, me % 2
    x = chip % ROW

    def at_chip(c):
        return {"ctx": c * 2 + core}

    below = at_chip(lax.rem(chip + ROW, chips))
    above = at_chip(lax.rem(chip + chips - ROW, chips))
    peers = [at_chip(chip - x + lax.rem(x + j, ROW)) for j in range(1, ROW)]
    ahead_two = at_chip(lax.rem(chip + 2, chips))
    behind_two = at_chip(lax.rem(chip + chips - 2, chips))
    sibling = {"ctx": chip * 2 + (1 - core)}
    right = {"head": lax.rem(z + 1, planes)}
    left = {"head": lax.rem(z + planes - 1, planes)}

    loads = [
        pltpu.make_async_copy(src, dst, load_sem.at[i])
        for i, (src, dst) in enumerate(((q_hbm, q), (k_hbm, k_own), (v_hbm, v_own), (w_hbm, w)))
    ]
    for c in (loads[1], loads[2], loads[0]):
        c.start()

    barrier = pltpu.get_barrier_semaphore()
    sources = [above, *peers, behind_two, sibling, left, right]
    for d in sources:
        pl.semaphore_signal(barrier, inc=1, device_id=d, device_id_type=MESH)
    pl.semaphore_wait(barrier, len(sources))

    part = tok // PIECES
    pieces = range(2 * PIECES)

    def piece(refs, i, *at):
        return refs[i // PIECES].at[(*at, pl.ds(i % PIECES * part, part))]

    def send(i, src, slot, sem, to):
        return pltpu.make_async_remote_copy(
            src_ref=src, dst_ref=piece((kb, vb), i, slot), send_sem=kv_send.at[i, sem],
            recv_sem=kv_recv.at[i, slot], device_id=to, device_id_type=MESH)

    def own(i):
        return piece((k_hbm, v_hbm), i)

    def arrive(i, slot):
        send(i, own(i), slot, 0, sibling).wait_recv()

    def from_chip(i, j):
        arrive(i, SAME[j])
        send(i, piece((kb, vb), i, SAME[j]), SAME[j] + 1, 5 + j, sibling).start()

    for i in pieces:
        send(i, own(i), SAME[4], 0, below).start()
        for j in (1, 3, 2):
            @pl.when(x + j < ROW)
            def _():
                send(i, own(i), SAME[j], j, peers[j - 1]).start()

    @pl.when(x == ROW - 2)
    def _():
        for i in pieces:
            send(i, own(i), SAME[2], 2, ahead_two).start()

    @pl.when(x == ROW - 1)
    def _():
        for i in pieces[PIECES:]:
            send(i, own(i), SAME[2], 2, ahead_two).start()

    for i in pieces:
        send(i, own(i), MATE, 5, sibling).start()

    loads[3].start()

    lens = len_ref[...]
    docs = lens.shape[1]
    i0 = lax.broadcasted_iota(jnp.int32, (docs, docs), 0)
    i1 = lax.broadcasted_iota(jnp.int32, (docs, docs), 1)
    wide = jnp.broadcast_to(lens, (docs, docs))
    col = jnp.sum(jnp.where(i0 == i1, wide, 0), axis=1, keepdims=True)
    ends = jnp.sum(jnp.where(i0 <= i1, jnp.broadcast_to(col, (docs, docs)), 0), axis=0, keepdims=True)
    pos = me * tok + lax.broadcasted_iota(jnp.int32, (tok, docs), 0)
    ends = jnp.broadcast_to(ends, (tok, docs))
    began = jnp.max(jnp.where(ends <= pos, ends, 0), axis=1, keepdims=True)
    first[...] = jnp.broadcast_to(began, (tok, HEAD_SIZE))

    spread = tok // HEAD_SIZE

    def limits(r0, m, bases, causal):
        parts = []
        lane = lax.broadcasted_iota(jnp.int32, (m, tok), 1)
        for base in bases:
            ok = lane >= jnp.concatenate([first[r0:r0 + m, :] - base] * spread, axis=1)
            if causal:
                ok = ok & (lane <= lax.broadcasted_iota(jnp.int32, (m, tok), 0))
            parts.append(jnp.where(ok, jnp.float32(-MASKED), jnp.float32(MASKED)))
        return parts[0] if len(parts) == 1 else jnp.concatenate(parts, axis=1)

    def attend(r0, m, keys, vals, limit, fresh):
        wide = keys.shape[0]
        vals = jnp.concatenate([vals, jnp.ones((wide, HEAD_SIZE), jnp.bfloat16)], axis=1)
        span = slice(r0, r0 + m)

        def score(h):
            return lax.dot_general(q[span, h * HEAD_SIZE:(h + 1) * HEAD_SIZE], keys, (((1,), (1,)), ((), ())),
                                   preferred_element_type=jnp.float32)

        ahead = score(0)
        for h in range(heads):
            s = ahead
            if h + 1 < heads:
                ahead = score(h + 1)
            s = jnp.minimum(s, limit[...])
            new = jnp.broadcast_to(jnp.max(s, axis=1, keepdims=True), (m, HEAD_SIZE))
            if not fresh:
                old = top[h, span, :]
                new = jnp.maximum(old, new)
            p = jnp.exp2((s - jnp.concatenate([new] * (wide // HEAD_SIZE), axis=1)) * SCALE)
            both = jnp.dot(p.astype(jnp.bfloat16), vals, preferred_element_type=jnp.float32)
            if fresh:
                acc[h, span, :] = both
            else:
                fade = jnp.exp2((old - new) * SCALE)
                acc[h, span, :] = acc[h, span, :] * jnp.concatenate([fade, fade], axis=1) + both
            top[h, span, :] = new

    for c in loads[:3]:
        c.wait()
    bias[...] = limits(0, tok, [me * tok], True)
    attend(0, tok, k_own[...], v_own[...], bias, True)

    for i in pieces:
        arrive(i, SAME[4])
        for j in (1, 3, 2)[:3 if i < PIECES else 2]:
            @pl.when((x + j >= ROW) if j != 2 else (x == ROW - 1))
            def _():
                send(i, piece((kb, vb), i, SAME[4]), SAME[j], j, peers[j - 1]).start()
    for i in pieces:
        send(i, piece((kb, vb), i, SAME[4]), SAME[4] + 1, 9, sibling).start()
    for i in pieces:
        arrive(i, MATE)
        arrive(i, SAME[4] + 1)

    def far(n, carry):
        mine = jnp.where(core == 1, MATE, SAME[4] + 1)
        slot = jnp.where(n == 0, SAME[4], mine)
        block = jnp.where(n == 0, (chip - 4) * 2 + core, jnp.where(core == 1, chip * 2, (chip - 4) * 2 + 1))
        bias[...] = limits(0, tok, [block * tok], False)
        attend(0, tok, kb[slot], vb[slot], bias, False)
        return carry

    lax.fori_loop(0, 2, far, 0)
    for j in (1, 3, 2):
        for i in pieces:
            from_chip(i, j)

    def z_copy(src, t, slot, to):
        return pltpu.make_async_remote_copy(
            src_ref=src, dst_ref=gat.at[t, slot], send_sem=z_send.at[t, slot],
            recv_sem=z_recv.at[t, slot], device_id=to, device_id_type=MESH)

    last = planes - 2
    bases = [((chip - j) * 2 + c) * tok for j in (2, 3, 1) for c in (core, 1 - core)]

    def attend_slots(t, low, high):
        wide = (high - low) * tok
        limit = tail.at[:, low * tok:high * tok]
        limit[...] = limits(t * rows, rows, bases[low:high], False)
        attend(t * rows, rows, kb[low:high].reshape(wide, HEAD_SIZE), vb[low:high].reshape(wide, HEAD_SIZE), limit, False)

    for t in range(CHUNKS):
        if t == 0:
            for i in pieces:
                arrive(i, SAME[1] + 1)
            attend_slots(t, 4, 6)
            for i in pieces:
                arrive(i, SAME[3] + 1)
                arrive(i, SAME[2] + 1)
            attend_slots(t, 0, 4)
        else:
            attend_slots(t, 0, 6)
        span = pl.ds(t * rows, rows)
        for h in range(heads):
            num = acc[h, span, 0:HEAD_SIZE]
            den = acc[h, span, HEAD_SIZE:2 * HEAD_SIZE]
            att[t, :, h * HEAD_SIZE:(h + 1) * HEAD_SIZE] = (num / den).astype(jnp.bfloat16)
        z_copy(att.at[t], t, 0, right).start()
        z_copy(att.at[t], t, last, left).start()

    def weight(by):
        plane = lax.rem(z + planes - by, planes)
        return w[pl.ds(pl.multiple_of(plane * feat, feat), feat), :]

    loads[3].wait()
    for t in range(CHUNKS):
        total[pl.ds(t * rows, rows), :] = jnp.dot(att[t], weight(0), preferred_element_type=jnp.float32)

    def add(t, slot):
        total[pl.ds(t * rows, rows), :] += jnp.dot(
            gat[t, slot], weight(slot + 1), preferred_element_type=jnp.float32)

    def out_copy(t):
        span = pl.ds(t * rows, rows)
        return pltpu.make_async_copy(out.at[span], o_ref.at[span], out_sem.at[t])

    half = planes // 2
    for d in range(1, half + 1):
        for t in range(CHUNKS):
            far_right = half - t % 2
            far_left = planes - 1 - far_right
            if d <= far_right:
                z_copy(att.at[t], t, d - 1, right).wait_recv()
                if d < far_right:
                    z_copy(gat.at[t, d - 1], t, d, right).start()
            if d <= far_left:
                s = planes - 1 - d
                z_copy(att.at[t], t, s, left).wait_recv()
                if d < far_left:
                    z_copy(gat.at[t, s], t, s - 1, left).start()
            if d <= far_right:
                add(t, d - 1)
            if d <= far_left:
                add(t, planes - 1 - d)
            if d == half:
                span = pl.ds(t * rows, rows)
                out[span, :] = total[span, :].astype(out.dtype)
                out_copy(t).start()
    for t in range(CHUNKS):
        out_copy(t).wait()

    for i in pieces:
        for sem in (0, 1, 2, 3, 5, 6, 7, 8, 9):
            send(i, own(i), MATE, sem, sibling).wait_send()
    for t in range(CHUNKS):
        for slot in range(planes - 1):
            z_copy(att.at[t], t, slot, right).wait_send()


def shards(chips, planes, queries, keys, values, lengths, out_weight):
    tok, feat = queries.shape
    heads = feat // HEAD_SIZE
    bf, f32 = jnp.bfloat16, jnp.float32
    rows = tok // CHUNKS
    hbm = pl.BlockSpec(memory_space=pl.ANY)
    return pl.pallas_call(
        functools.partial(kernel, chips, planes),
        out_shape=jax.ShapeDtypeStruct((tok, out_weight.shape[1]), bf),
        in_specs=[pl.BlockSpec(memory_space=pltpu.VMEM), hbm, hbm, hbm, hbm],
        out_specs=hbm,
        scratch_shapes=[
            pltpu.VMEM((tok, feat), bf),
            pltpu.VMEM((tok, HEAD_SIZE), bf),
            pltpu.VMEM((tok, HEAD_SIZE), bf),
            pltpu.VMEM((9, tok, HEAD_SIZE), bf),
            pltpu.VMEM((9, tok, HEAD_SIZE), bf),
            pltpu.VMEM(out_weight.shape, bf),
            pltpu.VMEM((heads, tok, 2 * HEAD_SIZE), f32),
            pltpu.VMEM((heads, tok, HEAD_SIZE), f32),
            pltpu.VMEM((tok, HEAD_SIZE), jnp.int32),
            pltpu.VMEM((tok, tok), f32),
            pltpu.VMEM((rows, 6 * tok), f32),
            pltpu.VMEM((CHUNKS, rows, feat), bf),
            pltpu.VMEM((CHUNKS, planes - 1, rows, feat), bf),
            pltpu.VMEM((tok, out_weight.shape[1]), f32),
            pltpu.VMEM((tok, out_weight.shape[1]), bf),
            pltpu.SemaphoreType.DMA((4,)),
            pltpu.SemaphoreType.DMA((2 * PIECES, 10)),
            pltpu.SemaphoreType.DMA((2 * PIECES, 9)),
            pltpu.SemaphoreType.DMA((CHUNKS, planes - 1)),
            pltpu.SemaphoreType.DMA((CHUNKS, planes - 1)),
            pltpu.SemaphoreType.DMA((CHUNKS,)),
        ],
        compiler_params=pltpu.CompilerParams(
            collective_id=0, has_side_effects=True, vmem_limit_bytes=62 * 2**20),
    )(lengths.reshape(1, -1), queries, keys, values, out_weight)


def solution(mesh):
    return jax.shard_map(
        functools.partial(shards, mesh.shape["ctx"] // 2, mesh.shape["head"]),
        mesh=mesh,
        in_specs=(P("ctx", "head"), P("ctx", "head"), P("ctx", "head"), P(), P(None, "head")),
        out_specs=P("ctx", "head"),
        check_vma=False,
    )
```

```python
import functools
import math

import jax
import jax.numpy as jnp
from jax import lax
from jax.experimental import pallas as pl
from jax.experimental.pallas import tpu as pltpu
from jax.sharding import PartitionSpec as P

HEAD_SIZE = 128
SCALE = HEAD_SIZE ** -0.5 * math.log2(math.e)
MASKED = -1e30
CHUNKS = 4
ROW = 4
PIECES = 2
SAME = {2: 0, 3: 2, 1: 4, 4: 6}
MATE = 8
MESH = pl.DeviceIdType.MESH


def kernel(chips, planes, len_ref, q_hbm, k_hbm, v_hbm, w_hbm, o_ref,
           q, k_own, v_own, kb, vb, w, acc, top, first, bias, tail, att, gat, total, out,
           load_sem, kv_send, kv_recv, z_send, z_recv, out_sem):
    tok = q.shape[0]
    feat = q.shape[1]
    heads = feat // HEAD_SIZE
    rows = tok // CHUNKS
    me = lax.axis_index("ctx")
    z = lax.axis_index("head")
    chip, core = me // 2, me % 2
    x = chip % ROW

    def at_chip(c):
        return {"ctx": c * 2 + core}

    below = at_chip(lax.rem(chip + ROW, chips))
    above = at_chip(lax.rem(chip + chips - ROW, chips))
    peers = [at_chip(chip - x + lax.rem(x + j, ROW)) for j in range(1, ROW)]
    ahead_two = at_chip(lax.rem(chip + 2, chips))
    behind_two = at_chip(lax.rem(chip + chips - 2, chips))
    sibling = {"ctx": chip * 2 + (1 - core)}
    right = {"head": lax.rem(z + 1, planes)}
    left = {"head": lax.rem(z + planes - 1, planes)}

    loads = [
        pltpu.make_async_copy(src, dst, load_sem.at[i])
        for i, (src, dst) in enumerate(((q_hbm, q), (k_hbm, k_own), (v_hbm, v_own), (w_hbm, w)))
    ]
    for c in (loads[1], loads[2], loads[0]):
        c.start()

    barrier = pltpu.get_barrier_semaphore()
    sources = [above, *peers, behind_two, sibling, left, right]
    for d in sources:
        pl.semaphore_signal(barrier, inc=1, device_id=d, device_id_type=MESH)
    pl.semaphore_wait(barrier, len(sources))

    part = tok // PIECES
    pieces = range(2 * PIECES)

    def piece(refs, i, *at):
        return refs[i // PIECES].at[(*at, pl.ds(i % PIECES * part, part))]

    def send(i, src, slot, sem, to):
        return pltpu.make_async_remote_copy(
            src_ref=src, dst_ref=piece((kb, vb), i, slot), send_sem=kv_send.at[i, sem],
            recv_sem=kv_recv.at[i, slot], device_id=to, device_id_type=MESH)

    def own(i):
        return piece((k_hbm, v_hbm), i)

    def arrive(i, slot):
        send(i, own(i), slot, 0, sibling).wait_recv()

    def from_chip(i, j):
        arrive(i, SAME[j])
        send(i, piece((kb, vb), i, SAME[j]), SAME[j] + 1, 5 + j, sibling).start()

    for i in pieces:
        send(i, own(i), SAME[4], 0, below).start()
        for j in (1, 3, 2):
            @pl.when(x + j < ROW)
            def _():
                send(i, own(i), SAME[j], j, peers[j - 1]).start()

    @pl.when(x == ROW - 2)
    def _():
        for i in pieces:
            send(i, own(i), SAME[2], 2, ahead_two).start()

    @pl.when(x == ROW - 1)
    def _():
        for i in pieces[PIECES:]:
            send(i, own(i), SAME[2], 2, ahead_two).start()

    for i in pieces:
        send(i, own(i), MATE, 5, sibling).start()

    loads[3].start()

    lens = len_ref[...]
    docs = lens.shape[1]
    i0 = lax.broadcasted_iota(jnp.int32, (docs, docs), 0)
    i1 = lax.broadcasted_iota(jnp.int32, (docs, docs), 1)
    wide = jnp.broadcast_to(lens, (docs, docs))
    col = jnp.sum(jnp.where(i0 == i1, wide, 0), axis=1, keepdims=True)
    ends = jnp.sum(jnp.where(i0 <= i1, jnp.broadcast_to(col, (docs, docs)), 0), axis=0, keepdims=True)
    pos = me * tok + lax.broadcasted_iota(jnp.int32, (tok, docs), 0)
    ends = jnp.broadcast_to(ends, (tok, docs))
    began = jnp.max(jnp.where(ends <= pos, ends, 0), axis=1, keepdims=True)
    first[...] = jnp.broadcast_to(began, (tok, HEAD_SIZE))

    spread = tok // HEAD_SIZE

    def limits(r0, m, bases, causal):
        parts = []
        lane = lax.broadcasted_iota(jnp.int32, (m, tok), 1)
        for base in bases:
            ok = lane >= jnp.concatenate([first[r0:r0 + m, :] - base] * spread, axis=1)
            if causal:
                ok = ok & (lane <= lax.broadcasted_iota(jnp.int32, (m, tok), 0))
            parts.append(jnp.where(ok, jnp.float32(-MASKED), jnp.float32(MASKED)))
        return parts[0] if len(parts) == 1 else jnp.concatenate(parts, axis=1)

    def attend(r0, m, keys, vals, limit, fresh):
        wide = keys.shape[0]
        vals = jnp.concatenate([vals, jnp.ones((wide, HEAD_SIZE), jnp.bfloat16)], axis=1)
        span = slice(r0, r0 + m)

        def score(h):
            return lax.dot_general(q[span, h * HEAD_SIZE:(h + 1) * HEAD_SIZE], keys, (((1,), (1,)), ((), ())),
                                   preferred_element_type=jnp.float32)

        ahead = score(0)
        for h in range(heads):
            s = ahead
            if h + 1 < heads:
                ahead = score(h + 1)
            s = jnp.minimum(s, limit[...])
            new = jnp.broadcast_to(jnp.max(s, axis=1, keepdims=True), (m, HEAD_SIZE))
            if not fresh:
                old = top[h, span, :]
                new = jnp.maximum(old, new)
            p = jnp.exp2((s - jnp.concatenate([new] * (wide // HEAD_SIZE), axis=1)) * SCALE)
            both = jnp.dot(p.astype(jnp.bfloat16), vals, preferred_element_type=jnp.float32)
            if fresh:
                acc[h, span, :] = both
            else:
                fade = jnp.exp2((old - new) * SCALE)
                acc[h, span, :] = acc[h, span, :] * jnp.concatenate([fade, fade], axis=1) + both
            top[h, span, :] = new

    for c in loads[:3]:
        c.wait()
    bias[...] = limits(0, tok, [me * tok], True)
    attend(0, tok, k_own[...], v_own[...], bias, True)

    for i in pieces:
        arrive(i, SAME[4])
        for j in (1, 3, 2)[:3 if i < PIECES else 2]:
            @pl.when((x + j >= ROW) if j != 2 else (x == ROW - 1))
            def _():
                send(i, piece((kb, vb), i, SAME[4]), SAME[j], j, peers[j - 1]).start()
    for i in pieces:
        send(i, piece((kb, vb), i, SAME[4]), SAME[4] + 1, 9, sibling).start()
    for i in pieces:
        arrive(i, MATE)
        arrive(i, SAME[4] + 1)

    def far(n, carry):
        mine = jnp.where(core == 1, MATE, SAME[4] + 1)
        slot = jnp.where(n == 0, SAME[4], mine)
        block = jnp.where(n == 0, (chip - 4) * 2 + core, jnp.where(core == 1, chip * 2, (chip - 4) * 2 + 1))
        bias[...] = limits(0, tok, [block * tok], False)
        attend(0, tok, kb[slot], vb[slot], bias, False)
        return carry

    lax.fori_loop(0, 2, far, 0)
    for j in (2, 1):
        for i in pieces:
            from_chip(i, j)

    def z_copy(src, t, slot, to):
        return pltpu.make_async_remote_copy(
            src_ref=src, dst_ref=gat.at[t, slot], send_sem=z_send.at[t, slot],
            recv_sem=z_recv.at[t, slot], device_id=to, device_id_type=MESH)

    last = planes - 2
    bases = [((chip - j) * 2 + c) * tok for j in (2, 3, 1) for c in (core, 1 - core)]

    def attend_slots(t, low, high):
        wide = (high - low) * tok
        limit = tail.at[:, low * tok:high * tok]
        limit[...] = limits(t * rows, rows, bases[low:high], False)
        attend(t * rows, rows, kb[low:high].reshape(wide, HEAD_SIZE), vb[low:high].reshape(wide, HEAD_SIZE), limit, False)

    for t in range(CHUNKS):
        if t == 0:
            for i in pieces:
                arrive(i, SAME[2] + 1)
            attend_slots(t, 0, 2)
            for i in pieces:
                from_chip(i, 3)
            for i in pieces:
                arrive(i, SAME[1] + 1)
            attend_slots(t, 4, 6)
            attend_slots(t, 2, 3)
            for i in pieces:
                arrive(i, SAME[3] + 1)
            attend_slots(t, 3, 4)
        else:
            attend_slots(t, 0, 6)
        span = pl.ds(t * rows, rows)
        for h in range(heads):
            num = acc[h, span, 0:HEAD_SIZE]
            den = acc[h, span, HEAD_SIZE:2 * HEAD_SIZE]
            att[t, :, h * HEAD_SIZE:(h + 1) * HEAD_SIZE] = (num / den).astype(jnp.bfloat16)
        z_copy(att.at[t], t, 0, right).start()
        z_copy(att.at[t], t, last, left).start()

    def weight(by):
        plane = lax.rem(z + planes - by, planes)
        return w[pl.ds(pl.multiple_of(plane * feat, feat), feat), :]

    loads[3].wait()
    for t in range(CHUNKS):
        total[pl.ds(t * rows, rows), :] = jnp.dot(att[t], weight(0), preferred_element_type=jnp.float32)

    def add(t, slot):
        total[pl.ds(t * rows, rows), :] += jnp.dot(
            gat[t, slot], weight(slot + 1), preferred_element_type=jnp.float32)

    def out_copy(t):
        span = pl.ds(t * rows, rows)
        return pltpu.make_async_copy(out.at[span], o_ref.at[span], out_sem.at[t])

    half = planes // 2
    for d in range(1, half + 1):
        for t in range(CHUNKS):
            far_right = half - t % 2
            far_left = planes - 1 - far_right
            if d <= far_right:
                z_copy(att.at[t], t, d - 1, right).wait_recv()
                if d < far_right:
                    z_copy(gat.at[t, d - 1], t, d, right).start()
            if d <= far_left:
                s = planes - 1 - d
                z_copy(att.at[t], t, s, left).wait_recv()
                if d < far_left:
                    z_copy(gat.at[t, s], t, s - 1, left).start()
            if d <= far_right:
                add(t, d - 1)
            if d <= far_left:
                add(t, planes - 1 - d)
            if d == half:
                span = pl.ds(t * rows, rows)
                out[span, :] = total[span, :].astype(out.dtype)
                out_copy(t).start()
    for t in range(CHUNKS):
        out_copy(t).wait()

    for i in pieces:
        for sem in (0, 1, 2, 3, 5, 6, 7, 8, 9):
            send(i, own(i), MATE, sem, sibling).wait_send()
    for t in range(CHUNKS):
        for slot in range(planes - 1):
            z_copy(att.at[t], t, slot, right).wait_send()


def shards(chips, planes, queries, keys, values, lengths, out_weight):
    tok, feat = queries.shape
    heads = feat // HEAD_SIZE
    bf, f32 = jnp.bfloat16, jnp.float32
    rows = tok // CHUNKS
    hbm = pl.BlockSpec(memory_space=pl.ANY)
    return pl.pallas_call(
        functools.partial(kernel, chips, planes),
        out_shape=jax.ShapeDtypeStruct((tok, out_weight.shape[1]), bf),
        in_specs=[pl.BlockSpec(memory_space=pltpu.VMEM), hbm, hbm, hbm, hbm],
        out_specs=hbm,
        scratch_shapes=[
            pltpu.VMEM((tok, feat), bf),
            pltpu.VMEM((tok, HEAD_SIZE), bf),
            pltpu.VMEM((tok, HEAD_SIZE), bf),
            pltpu.VMEM((9, tok, HEAD_SIZE), bf),
            pltpu.VMEM((9, tok, HEAD_SIZE), bf),
            pltpu.VMEM(out_weight.shape, bf),
            pltpu.VMEM((heads, tok, 2 * HEAD_SIZE), f32),
            pltpu.VMEM((heads, tok, HEAD_SIZE), f32),
            pltpu.VMEM((tok, HEAD_SIZE), jnp.int32),
            pltpu.VMEM((tok, tok), f32),
            pltpu.VMEM((rows, 6 * tok), f32),
            pltpu.VMEM((CHUNKS, rows, feat), bf),
            pltpu.VMEM((CHUNKS, planes - 1, rows, feat), bf),
            pltpu.VMEM((tok, out_weight.shape[1]), f32),
            pltpu.VMEM((tok, out_weight.shape[1]), bf),
            pltpu.SemaphoreType.DMA((4,)),
            pltpu.SemaphoreType.DMA((2 * PIECES, 10)),
            pltpu.SemaphoreType.DMA((2 * PIECES, 9)),
            pltpu.SemaphoreType.DMA((CHUNKS, planes - 1)),
            pltpu.SemaphoreType.DMA((CHUNKS, planes - 1)),
            pltpu.SemaphoreType.DMA((CHUNKS,)),
        ],
        compiler_params=pltpu.CompilerParams(
            collective_id=0, has_side_effects=True, vmem_limit_bytes=62 * 2**20),
    )(lengths.reshape(1, -1), queries, keys, values, out_weight)


def solution(mesh):
    return jax.shard_map(
        functools.partial(shards, mesh.shape["ctx"] // 2, mesh.shape["head"]),
        mesh=mesh,
        in_specs=(P("ctx", "head"), P("ctx", "head"), P("ctx", "head"), P(), P(None, "head")),
        out_specs=P("ctx", "head"),
        check_vma=False,
    )
```
